32 devices in a mesh: groups: 2 (over y), branch: 4 (over z), rhs: 2 (over x), inner: 2 (over core).
Axes of the slice: x: 2, y: 2, z: 4, core: 2. Of those that a mesh axis runs over, the one named last changes fastest.
Arguments:
- vectors: float32 [32, 16384], P('rhs', ('groups', 'branch', 'inner')), parts along dimension 1, may hold values from -6 to 6
- leaf_basis: float32 [64, 16384], P(None, ('groups', 'branch', 'inner')), parts along dimension 1, may hold values from -0.75 to 0.75
- near_blocks: float32 [3, 64, 16384], P(None, None, ('groups', 'branch', 'inner')), parts along dimension 2, may hold values from -0.4375 to 0.4375
- transfer: float32 [64, 31744], P(None, ('groups', 'branch', 'inner')), parts along dimension 1, may hold values from -0.5 to 0.5
- coupling: float32 [64, 63488], P(None, ('groups', 'branch', 'inner')), parts along dimension 1, may hold values from -0.5 to 0.5
- coupling_source: int32 [496, 2], P(('groups', 'branch', 'inner')), parts along dimension 0, may hold values from 0 to 127, as said below
- top_transfer: float32 [64, 512], P(None, 'groups'), parts along dimension 1, may hold values from -0.5 to 0.5
- upper_coupling_matrices: float32 [64, 2048], P(None, ('groups', 'branch')), parts along dimension 1, may hold values from -0.5 to 0.5
- top_target: int32 [32], P(('groups', 'branch')), parts along dimension 0, may hold values from 0 to 5, as said below
- top_source: int32 [32], P(('groups', 'branch')), parts along dimension 0, may hold values from 0 to 5, as said below
Outputs:
- product: float32 [32, 16384], P('rhs', ('groups', 'branch', 'inner')), parts along dimension 1
The draws below stay inside these ranges and needn't reach their ends.
There are 2 independent parts, one for each index of `groups`. The reference program is written for one: setup_inputs(seed, part) draws one part's arguments, and reference() takes and returns one part's arrays. A program takes and returns all parts, laid end to end along the dimension named above; each array names one. Nothing has to cross between parts.
Inputs may be any that keep to these rules, and one draw needn't show every extreme that they name: `coupling_source`: the partner of lower cluster c of a level with w = 16 / 2^h clusters per run lies in the same run of w clusters as c or in the run just before or after it (runs are c div w); a run at either end has no run beyond it. `top_target`: pairs alternate in level: even pairs join two different branch clusters (ids below 4), odd pairs two different clusters of the next level (ids 4 and above). `top_source`: same level as the pair's target and never equal to it.
All inputs are finite; a program needn't handle non-finite values.
Results may differ from the reference program's by a relative error of at most 0.0001.
Values sent between devices are 32-bit elements; how exact they have to be, the bound alone decides.
A program may use at most 64 MiB of HBM per device.

```python
import jax
import jax.numpy as jnp
from jax import lax

BASIS_RANK = 64
LEAF = 64
RHS = 32
PARTNERS = 2
TOPSLOT = 4
LEAF_DEV = 16
NPTS = 8192
NCLUSTERS = 248
UPPER_PAIR_COUNT = 16
N_BRANCH = 4
N_INNER = 2


def draw_coupling_source(key, part):
    key = jax.random.fold_in(key, 11)
    devices_all = N_BRANCH * N_INNER
    clusters = 2 * LEAF_DEV - 1
    levels = LEAF_DEV.bit_length() - 1
    cluster_ids = jnp.arange(clusters, dtype=jnp.int32)
    heights = jnp.zeros((clusters,), jnp.int32)
    for height in range(1, levels + 1):
        heights = heights + (cluster_ids >= 2 * LEAF_DEV - 2 * (LEAF_DEV >> height)).astype(jnp.int32)
    breadth = jnp.right_shift(jnp.full((clusters,), LEAF_DEV, jnp.int32), heights)
    first_key, second_key = jax.random.split(key)
    shifts = jax.random.randint(first_key, (devices_all, clusters, PARTNERS), -1, 2)
    device_ids = jnp.arange(devices_all, dtype=jnp.int32)[:, None, None]
    source_dev = jnp.clip(device_ids + shifts, 0, devices_all - 1)
    limits = jnp.broadcast_to(breadth[None, :, None], (devices_all, clusters, PARTNERS))
    within = jax.random.randint(second_key, (devices_all, clusters, PARTNERS), 0, limits)
    result = source_dev * breadth[None, :, None] + within
    result = result.at[0, 0, 0].set(0)
    result = result.at[devices_all - 1, LEAF_DEV - 1, 0].set(devices_all * LEAF_DEV - 1)
    return result.reshape(devices_all * clusters, PARTNERS).astype(jnp.int32)


def top_pairs(key):
    first_key, second_key = jax.random.split(key)
    slots = N_BRANCH * TOPSLOT
    upper_half = jnp.arange(slots, dtype=jnp.int32) % 2
    counts = jnp.where(upper_half == 1, N_BRANCH // 2, N_BRANCH).astype(jnp.int32)
    first_id = upper_half * N_BRANCH
    target = jax.random.randint(first_key, (slots,), 0, counts)
    stride = jax.random.randint(second_key, (slots,), 1, counts)
    source = (target + stride) % counts
    target = first_id + target
    source = first_id + source
    final_upper_index = N_BRANCH + N_BRANCH // 2 - 1
    target = target.at[0].set(0).at[1].set(final_upper_index).at[2].set(1).at[3].set(N_BRANCH)
    source = source.at[0].set(1).at[1].set(N_BRANCH).at[2].set(0).at[3].set(final_upper_index)
    return (target.astype(jnp.int32), source.astype(jnp.int32))


def draw_top_target(key, part):
    target, source = top_pairs(key)
    return target


def draw_top_source(key, part):
    target, source = top_pairs(key)
    return source


def steps_of(rng, dims, cuts, least, top_value):
    factor_of = 1.0
    for dim, shards_of in cuts:
        draws = jax.random.uniform(jax.random.fold_in(jax.random.fold_in(rng, 6), dim), (shards_of,), jnp.float32, least / len(cuts), top_value / len(cuts))
        factor_of = factor_of * jnp.repeat(jnp.exp(draws), dims[dim] // shards_of).reshape((-1,) + (1,) * (len(dims) - 1 - dim))
    return factor_of


def centred(key, shape, deviation, limit, cuts=(), kind=jnp.bfloat16):
    loudness = steps_of(key, shape, cuts, -0.22, 0.18) if cuts else 1.0
    entries = jax.random.normal(key, shape, jnp.float32) * deviation * loudness
    return jnp.minimum(jnp.maximum(entries, -limit), limit).astype(kind)


def setup_inputs(seed: int = 0, part: int = 0) -> dict:
    arg_keys = jax.random.split(jax.random.key(seed), 11)
    part_splits = jax.random.split(jax.random.fold_in(arg_keys[10], part), 11)
    return {
        "vectors": centred(part_splits[0], (RHS, NPTS), 1.0, 6.0, ((0, 2), (1, 8)), jnp.float32),
        "leaf_basis": centred(part_splits[1], (BASIS_RANK, NPTS), LEAF ** -0.5, 0.75, ((1, 8),), jnp.float32),
        "near_blocks": centred(part_splits[2], (3, LEAF, NPTS), (3 * LEAF) ** -0.5, 0.4375, ((2, 8),), jnp.float32),
        "transfer": centred(part_splits[3], (BASIS_RANK, NCLUSTERS * BASIS_RANK), (2 * BASIS_RANK) ** -0.5, 0.5, ((1, 8),), jnp.float32),
        "coupling": centred(part_splits[4], (BASIS_RANK, NCLUSTERS * PARTNERS * BASIS_RANK), (PARTNERS * BASIS_RANK) ** -0.5, 0.5, ((1, 8),), jnp.float32),
        "coupling_source": draw_coupling_source(jax.random.fold_in(jax.random.fold_in(arg_keys[10], part), 71), part),
        "top_transfer": centred(part_splits[6], (BASIS_RANK, N_BRANCH * BASIS_RANK), (2 * BASIS_RANK) ** -0.5, 0.5, (), jnp.float32),
        "upper_coupling_matrices": centred(part_splits[7], (BASIS_RANK, UPPER_PAIR_COUNT * BASIS_RANK), (2 * BASIS_RANK) ** -0.5, 0.5, ((1, 4),), jnp.float32),
        "top_target": draw_top_target(jax.random.fold_in(jax.random.fold_in(arg_keys[10], part), 71), part),
        "top_source": draw_top_source(jax.random.fold_in(jax.random.fold_in(arg_keys[10], part), 71), part),
    }


EXACT = lax.Precision.HIGHEST


def reference(vectors, leaf_basis, near_blocks, transfer, coupling, coupling_source, top_transfer, upper_coupling_matrices, top_target, top_source):
    devices_all = N_BRANCH * N_INNER
    levels = LEAF_DEV.bit_length() - 1
    clusters = 2 * LEAF_DEV - 1
    leaf_total = devices_all * LEAF_DEV
    starts = [2 * LEAF_DEV - 2 * (LEAF_DEV >> height) for height in range(levels + 1)]
    blocks = vectors.reshape(RHS, leaf_total, LEAF)
    basis_blocks = leaf_basis.reshape(BASIS_RANK, leaf_total, LEAF)
    transfers = transfer.reshape(BASIS_RANK, devices_all, clusters, BASIS_RANK)
    coupling_factors = coupling.reshape(BASIS_RANK, devices_all, clusters, PARTNERS, BASIS_RANK)
    sources = coupling_source.reshape(devices_all, clusters, PARTNERS)
    coefs = [jnp.einsum("rti,cti->tcr", basis_blocks, blocks, precision=EXACT)]
    for height in range(levels):
        breadth = LEAF_DEV >> height
        moving = transfers[:, :, starts[height]:starts[height] + breadth].reshape(BASIS_RANK, devices_all * breadth, BASIS_RANK)
        lifted = jnp.einsum("aqb,qca->qcb", moving, coefs[height], precision=EXACT)
        coefs.append(lifted.reshape(devices_all * breadth // 2, 2, RHS, BASIS_RANK).sum(1))
    coupled = []
    for height in range(levels + 1):
        breadth = LEAF_DEV >> height
        slot_blocks = coupling_factors[:, :, starts[height]:starts[height] + breadth].reshape(BASIS_RANK, devices_all * breadth * PARTNERS, BASIS_RANK)
        picked = jnp.take(coefs[height], sources[:, starts[height]:starts[height] + breadth].reshape(-1), axis=0)
        terms = jnp.einsum("aqb,qcb->qca", slot_blocks, picked, precision=EXACT)
        coupled.append(terms.reshape(devices_all * breadth, PARTNERS, RHS, BASIS_RANK).sum(1))
    root_moves = transfers[:, :, clusters - 1]
    root_terms = jnp.einsum("aqb,qca->qcb", root_moves, coefs[levels], precision=EXACT)
    leading_upper_index = root_terms.reshape(N_BRANCH, N_INNER, RHS, BASIS_RANK).sum(1)
    top_moves = top_transfer.reshape(BASIS_RANK, N_BRANCH, BASIS_RANK)
    second_top = jnp.einsum("aqb,qca->qcb", top_moves, leading_upper_index, precision=EXACT)
    second_top = second_top.reshape(N_BRANCH // 2, 2, RHS, BASIS_RANK).sum(1)
    top_coef = jnp.concatenate([leading_upper_index, second_top], axis=0)
    chosen = jnp.take(top_coef, top_source, axis=0)
    slot_terms = jnp.einsum("aqb,qcb->qca", upper_coupling_matrices.reshape(BASIS_RANK, -1, BASIS_RANK), chosen, precision=EXACT)
    selector = (top_target[None, :] == jnp.arange(N_BRANCH + N_BRANCH // 2, dtype=jnp.int32)[:, None]).astype(jnp.float32)
    top_field = jnp.einsum("kq,qca->kca", selector, slot_terms, precision=EXACT)
    field_first = top_field[:N_BRANCH] + jnp.einsum("aqb,qcb->qca", top_moves, jnp.repeat(top_field[N_BRANCH:], 2, axis=0), precision=EXACT)
    fields = coupled[levels] + jnp.einsum("aqb,qcb->qca", root_moves, jnp.repeat(field_first, N_INNER, axis=0), precision=EXACT)
    for height in reversed(range(levels)):
        breadth = LEAF_DEV >> height
        moving = transfers[:, :, starts[height]:starts[height] + breadth].reshape(BASIS_RANK, devices_all * breadth, BASIS_RANK)
        fields = coupled[height] + jnp.einsum("aqb,qcb->qca", moving, jnp.repeat(fields, 2, axis=0), precision=EXACT)
    result = jnp.einsum("rti,tcr->cti", basis_blocks, fields, precision=EXACT)
    extended = jnp.pad(blocks, ((0, 0), (1, 1), (0, 0)))
    stencil = near_blocks.reshape(3, LEAF, leaf_total, LEAF)
    for offset in range(3):
        result = result + jnp.einsum("jti,ctj->cti", stencil[offset], extended[:, offset:offset + leaf_total], precision=EXACT)
    return result.reshape(RHS, leaf_total * LEAF)
```

```python
import functools

import jax
import jax.numpy as jnp
from jax import lax
from jax.experimental import pallas as pl
from jax.experimental.pallas import tpu as pltpu
from jax.sharding import PartitionSpec as P

MESH = pl.DeviceIdType.MESH
NN = (((1,), (0,)), ((), ()))
NT = (((1,), (1,)), ((), ()))


def split(x):
    high = x.astype(jnp.bfloat16)
    return high, (x - high.astype(jnp.float32)).astype(jnp.bfloat16)


def product(x, weights, form):
    rows = x.shape[0]
    high, low = split(x)
    both = jnp.concatenate([high, low], axis=0)
    first = lax.dot_general(both, weights[0], form, preferred_element_type=jnp.float32)
    second = lax.dot_general(high, weights[1], form, preferred_element_type=jnp.float32)
    return first[:rows] + (first[rows:] + second)


def kernel(
    nb, ni,
    vec_hbm, basis_hbm, near_hbm, trans_hbm, coup_hbm, top_hbm, upper_hbm,
    source_ref, target_ref, top_source_ref,
    out_ref,
    vec, basis, near, trans, coup, top, upper,
    halo_low, halo_high, tab_low, tab_self, tab_high, dup, roots, near_sum,
    basis_w, quad_w,
    local_sem, halo_send, halo_recv, leaf_send, leaf_recv, rest_send, rest_recv,
    root_send, root_recv, upper_send, upper_recv,
):
    cols, points = vec.shape
    rank = basis.shape[0]
    assert rank == 64 and near.shape[1] == 64
    wide = 2 * rank
    leaves = points // 64
    levels = leaves.bit_length() - 1
    starts = [2 * leaves - 2 * (leaves >> h) for h in range(levels + 1)]
    clusters = 2 * leaves - 1
    tiles = leaves
    half = leaves // 2
    slots = upper.shape[2] // rank
    n = nb * ni
    branch = lax.axis_index("branch")
    inner = lax.axis_index("inner")
    me = branch * ni + inner

    def place(index):
        return {"branch": index // ni, "inner": index % ni}

    loads = [
        pltpu.make_async_copy(vec_hbm, vec, local_sem.at[0]),
        pltpu.make_async_copy(basis_hbm, basis, local_sem.at[1]),
        pltpu.make_async_copy(upper_hbm, upper.at[branch, 0:rank], local_sem.at[2]),
        pltpu.make_async_copy(trans_hbm, trans, local_sem.at[3]),
        pltpu.make_async_copy(near_hbm, near, local_sem.at[4]),
        pltpu.make_async_copy(coup_hbm, coup, local_sem.at[5]),
        pltpu.make_async_copy(top_hbm, top, local_sem.at[6]),
    ]
    for load in loads:
        load.start()

    barrier = pltpu.get_barrier_semaphore()
    for step in range(1, n):
        pl.semaphore_signal(
            barrier, inc=1, device_id=place((me + step) % n), device_id_type=MESH
        )

    row = lax.broadcasted_iota(jnp.int32, (8, slots * rank), 0)
    lane = lax.broadcasted_iota(jnp.int32, (8, slots * rank), 1)
    meta = jnp.zeros((8, slots * rank), jnp.int32)
    for slot in range(slots):
        here = lane // rank == slot
        meta = jnp.where(here & (row == 0), target_ref[slot], meta)
        meta = jnp.where(here & (row == 1), top_source_ref[slot], meta)
    upper[branch, rank:, :] = meta.astype(jnp.float32)

    def to_high(source, target, send, recv):
        return pltpu.make_async_remote_copy(
            source, target, send.at[0], recv.at[0], device_id=place(me + 1), device_id_type=MESH
        )

    def to_low(source, target, send, recv):
        return pltpu.make_async_remote_copy(
            source, target, send.at[1], recv.at[1], device_id=place(me - 1), device_id_type=MESH
        )

    halo_copies = (
        to_high(vec.at[:, points - wide : points], halo_low, halo_send, halo_recv),
        to_low(vec.at[:, 0:wide], halo_high, halo_send, halo_recv),
    )
    leaf_copies = (
        to_high(tab_self.at[0:half], tab_low.at[0:half], leaf_send, leaf_recv),
        to_low(tab_self.at[0:half], tab_high.at[0:half], leaf_send, leaf_recv),
    )
    rest_copies = (
        to_high(tab_self.at[half:tiles], tab_low.at[half:tiles], rest_send, rest_recv),
        to_low(tab_self.at[half:tiles], tab_high.at[half:tiles], rest_send, rest_recv),
    )
    upper_copies = [
        pltpu.make_async_remote_copy(
            upper.at[branch], upper.at[branch], upper_send.at[step], upper_recv.at[step],
            device_id={"branch": (branch + step) % nb}, device_id_type=MESH,
        )
        for step in range(1, nb)
    ]
    root_copies = [
        pltpu.make_async_remote_copy(
            roots.at[me], roots.at[me], root_send.at[step], root_recv.at[step],
            device_id=place((me + step) % n), device_id_type=MESH,
        )
        for step in range(1, n)
    ]
    has_low = me > 0
    has_high = me < n - 1

    def start(copies):
        @pl.when(has_high)
        def _():
            copies[0].start()

        @pl.when(has_low)
        def _():
            copies[1].start()

    def arrived(copies):
        @pl.when(has_low)
        def _():
            copies[0].wait_recv()

        @pl.when(has_high)
        def _():
            copies[1].wait_recv()

    def sent(copies):
        @pl.when(has_high)
        def _():
            copies[0].wait_send()

        @pl.when(has_low)
        def _():
            copies[1].wait_send()

    low_64 = lax.broadcasted_iota(jnp.int32, (rank, wide), 1) < rank
    low_c = lax.broadcasted_iota(jnp.int32, (cols, wide), 1) < rank
    low_s = lax.broadcasted_iota(jnp.int32, (rank, 2 * wide), 1) < wide

    loads[0].wait()
    loads[1].wait()
    pairs = []
    for k in range(half):
        both = basis[:, k * wide : (k + 1) * wide]
        weights = split(
            jnp.concatenate([jnp.where(low_64, both, 0.0), jnp.where(low_64, 0.0, both)], axis=0)
        )
        basis_w[0, k] = weights[0]
        basis_w[1, k] = weights[1]
        pair = product(vec[:, k * wide : (k + 1) * wide], weights, NT)
        tab_self[k] = pair
        pairs.append(pair)

    pl.semaphore_wait(barrier, n - 1)
    start(halo_copies)
    start(leaf_copies)
    loads[2].wait()
    for copy in upper_copies:
        copy.start()

    loads[3].wait()
    quad = 0
    for h in range(levels - 1):
        breadth = leaves >> h
        base = starts[h] // 2
        lifted = []
        for j in range(breadth // 4):
            at = (base + 2 * j) * wide
            first = trans[:, at : at + wide]
            second = trans[:, at + wide : at + 2 * wide]
            weights = split(
                jnp.concatenate(
                    [
                        jnp.where(low_64, first, 0.0),
                        jnp.where(low_64, pltpu.roll(first, rank, 1), 0.0),
                        jnp.where(low_64, 0.0, pltpu.roll(second, rank, 1)),
                        jnp.where(low_64, 0.0, second),
                    ],
                    axis=0,
                )
            )
            quad_w[0, quad] = weights[0]
            quad_w[1, quad] = weights[1]
            quad += 1
            pair = product(
                jnp.concatenate([pairs[2 * j], pairs[2 * j + 1]], axis=1), weights, NN
            )
            tab_self[starts[h + 1] // 2 + j] = pair
            lifted.append(pair)
        pairs = lifted
    at = starts[levels - 1] * rank
    both = trans[:, at : at + wide]
    last_w = split(
        jnp.concatenate(
            [jnp.where(low_64, both, 0.0), jnp.where(low_64, pltpu.roll(both, rank, 1), 0.0)],
            axis=0,
        )
    )
    single = product(pairs[0], last_w, NN)
    tab_self[tiles - 1] = single
    root = trans[:, (clusters - 1) * rank : clusters * rank]
    root = jnp.concatenate([root, root], axis=1)
    root_w = split(jnp.concatenate([root, root], axis=0))
    roots[me] = product(single, root_w, NN)
    for copy in root_copies:
        copy.start()
    start(rest_copies)

    loads[4].wait()
    arrived(halo_copies)
    turned = [pltpu.roll(vec[:, k * wide : (k + 1) * wide], rank, 1) for k in range(half)]
    before = jnp.where(has_low, pltpu.roll(halo_low[...], rank, 1), 0.0)
    after = jnp.where(has_high, pltpu.roll(halo_high[...], rank, 1), 0.0)
    turned = [before] + turned + [after]
    shifted = [jnp.where(low_c, turned[k], turned[k + 1]) for k in range(half + 1)]
    for k in range(half):
        lanes = slice(k * wide, (k + 1) * wide)
        lower, middle, higher = near[0, :, lanes], near[1, :, lanes], near[2, :, lanes]
        weights = split(
            jnp.concatenate(
                [
                    jnp.where(low_64, lower, 0.0),
                    jnp.where(low_64, middle, lower),
                    jnp.where(low_64, higher, middle),
                    jnp.where(low_64, 0.0, higher),
                ],
                axis=0,
            )
        )
        near_sum[:, lanes] = product(
            jnp.concatenate([shifted[k], shifted[k + 1]], axis=1), weights, NN
        )

    def both_ways(table, offset):
        for k in range(tiles):
            tile = table[k]
            dup[offset + 2 * k] = tile
            dup[offset + 2 * k + 1] = pltpu.roll(tile, rank, 1)

    both_ways(tab_self, 2 * tiles)
    arrived(leaf_copies)
    arrived(rest_copies)

    @pl.when(has_low)
    def _():
        both_ways(tab_low, 0)

    @pl.when(has_high)
    def _():
        both_ways(tab_high, 4 * tiles)

    loads[5].wait()

    def gathered(q):
        h = max(i for i in range(levels + 1) if starts[i] <= q)
        shift = levels - h

        def entry(slot):
            c = source_ref[q, slot]
            run = lax.shift_right_logical(c, shift)
            side = jnp.clip(run - me + 1, 0, 2)
            return side * (2 * tiles) + starts[h] + (c - lax.shift_left(run, shift))

        second = entry(1)
        second = second + 1 - 2 * (second & 1)
        return jnp.where(low_c, dup[entry(0)], dup[second])

    coupled = []
    for k in range(tiles - 1):
        both = coup[:, 2 * k * wide : 2 * (k + 1) * wide]
        weights = split(
            jnp.concatenate([jnp.where(low_s, both, 0.0), jnp.where(low_s, 0.0, both)], axis=0)
        )
        x = jnp.concatenate([gathered(2 * k), gathered(2 * k + 1)], axis=1)
        coupled.append(product(x, weights, NT))
    one = coup[:, (clusters - 1) * wide : clusters * wide]
    coupled.append(
        product(gathered(clusters - 1), split(jnp.concatenate([one, one], axis=0)), NT)
    )

    loads[6].wait()
    top_w = []
    for k in range(nb // 2):
        both = top[:, k * wide : (k + 1) * wide]
        other = pltpu.roll(both, rank, 1)
        top_w.append(
            split(
                jnp.concatenate(
                    [jnp.where(low_64, both, other), jnp.where(low_64, other, both)], axis=0
                )
            )
        )
    own = top[:, pl.ds(pl.multiple_of((branch // 2) * wide, wide), wide)]
    own_w = split(jnp.concatenate([own, own], axis=0))
    for copy in upper_copies:
        copy.wait_recv()
    upper_w = []
    for s in range(nb):
        block = upper[s, 0:rank, :]
        upper_w.append(split(jnp.concatenate([block, block], axis=0)))
    for copy in root_copies:
        copy.wait_recv()
    xu = []
    for g in range(nb):
        total = roots[g * ni]
        for i in range(1, ni):
            total = total + roots[g * ni + i]
        xu.append(total)
    for k in range(nb // 2):
        xu.append(product(jnp.where(low_c, xu[2 * k], xu[2 * k + 1]), top_w[k], NN))
    xu = [jnp.concatenate([x] * (slots * rank // wide), axis=1) for x in xu]
    field = jnp.zeros((2 * cols, wide), jnp.float32)
    first_id = branch.astype(jnp.float32)
    second_id = (nb + branch // 2).astype(jnp.float32)
    for s in range(nb):
        target = upper[s, rank : rank + 1, :]
        source = upper[s, rank + 1 : rank + 2, :]
        chosen = jnp.zeros((cols, slots * rank), jnp.float32)
        for k, x in enumerate(xu):
            chosen = jnp.where(source == float(k), x, chosen)
        x = jnp.concatenate(
            [
                jnp.where(target == first_id, chosen, 0.0),
                jnp.where(target == second_id, chosen, 0.0),
            ],
            axis=0,
        )
        field = field + product(x, upper_w[s], NT)
    side = lax.broadcasted_iota(jnp.int32, (cols, wide), 1) // rank == branch % 2
    own_field = field[:cols] + product(jnp.where(side, field[cols:], 0.0), own_w, NT)

    state = coupled[tiles - 1] + product(jnp.where(low_c, own_field, 0.0), root_w, NT)
    pairs = [coupled[starts[levels - 1] // 2] + product(state, last_w, NT)]
    for h in reversed(range(levels - 1)):
        count = (leaves >> h) // 4
        quad -= count
        base = starts[h] // 2
        lowered = []
        for j in range(count):
            moved = product(pairs[j], (quad_w[0, quad + j], quad_w[1, quad + j]), NT)
            lowered.append(coupled[base + 2 * j] + moved[:, :wide])
            lowered.append(coupled[base + 2 * j + 1] + moved[:, wide:])
        pairs = lowered
    for k in range(half):
        lanes = slice(k * wide, (k + 1) * wide)
        out_ref[:, lanes] = near_sum[:, lanes] + product(
            pairs[k], (basis_w[0, k], basis_w[1, k]), NN
        )

    sent(halo_copies)
    sent(leaf_copies)
    sent(rest_copies)
    for copy in upper_copies + root_copies:
        copy.wait_send()


def on_device(
    vectors,
    leaf_basis,
    near_blocks,
    transfer,
    coupling,
    coupling_source,
    top_transfer,
    upper_coupling_matrices,
    top_target,
    top_source,
):
    cols, points = vectors.shape
    rank = leaf_basis.shape[0]
    leaf_len = near_blocks.shape[1]
    leaves = points // leaf_len
    nb = lax.axis_size("branch")
    ni = lax.axis_size("inner")
    n = nb * ni
    quads = sum((leaves >> h) // 4 for h in range(leaves.bit_length() - 2))
    wide = 2 * rank
    f32, bf16 = jnp.float32, jnp.bfloat16
    dma = pltpu.SemaphoreType.DMA
    hbm = pl.BlockSpec(memory_space=pl.ANY)
    smem = pl.BlockSpec(memory_space=pltpu.SMEM)
    table = pltpu.VMEM((leaves, cols, wide), f32)
    halo = pltpu.VMEM((cols, wide), f32)
    return pl.pallas_call(
        functools.partial(kernel, nb, ni),
        out_shape=jax.ShapeDtypeStruct((cols, points), f32),
        in_specs=[hbm] * 7 + [smem] * 3,
        out_specs=pl.BlockSpec(memory_space=pltpu.VMEM),
        scratch_shapes=[
            pltpu.VMEM(vectors.shape, f32),
            pltpu.VMEM(leaf_basis.shape, f32),
            pltpu.VMEM(near_blocks.shape, f32),
            pltpu.VMEM(transfer.shape, f32),
            pltpu.VMEM(coupling.shape, f32),
            pltpu.VMEM(top_transfer.shape, f32),
            pltpu.VMEM((nb, rank + 8, upper_coupling_matrices.shape[1]), f32),
            halo,
            halo,
            table,
            table,
            table,
            pltpu.VMEM((6 * leaves, cols, wide), f32),
            pltpu.VMEM((n, cols, wide), f32),
            pltpu.VMEM((cols, points), f32),
            pltpu.VMEM((2, leaves // 2, wide, wide), bf16),
            pltpu.VMEM((2, quads, 2 * wide, wide), bf16),
            dma((7,)),
            dma((2,)),
            dma((2,)),
            dma((2,)),
            dma((2,)),
            dma((2,)),
            dma((2,)),
            dma((n,)),
            dma((n,)),
            dma((nb,)),
            dma((nb,)),
        ],
        compiler_params=pltpu.CompilerParams(
            collective_id=0, has_side_effects=True, vmem_limit_bytes=32 * 1024 * 1024
        ),
    )(
        vectors,
        leaf_basis,
        near_blocks,
        transfer,
        coupling,
        top_transfer,
        upper_coupling_matrices,
        coupling_source,
        top_target,
        top_source,
    )


def solution(mesh):
    placed = (
        P("rhs", ("groups", "branch", "inner")),
        P(None, ("groups", "branch", "inner")),
        P(None, None, ("groups", "branch", "inner")),
        P(None, ("groups", "branch", "inner")),
        P(None, ("groups", "branch", "inner")),
        P(("groups", "branch", "inner"), None),
        P(None, "groups"),
        P(None, ("groups", "branch")),
        P(("groups", "branch")),
        P(("groups", "branch")),
    )
    return jax.shard_map(
        on_device,
        mesh=mesh,
        in_specs=placed,
        out_specs=P("rhs", ("groups", "branch", "inner")),
        check_vma=False,
    )
```

```python
import functools

import jax
import jax.numpy as jnp
from jax import lax
from jax.experimental import pallas as pl
from jax.experimental.pallas import tpu as pltpu
from jax.sharding import PartitionSpec as P

MESH = pl.DeviceIdType.MESH
NN = (((1,), (0,)), ((), ()))
NT = (((1,), (1,)), ((), ()))


def split(x):
    high = x.astype(jnp.bfloat16)
    return high, (x - high.astype(jnp.float32)).astype(jnp.bfloat16)


def product(x, weights, form):
    rows = x.shape[0]
    high, low = split(x)
    both = jnp.concatenate([high, low], axis=0)
    first = lax.dot_general(both, weights[0], form, preferred_element_type=jnp.float32)
    second = lax.dot_general(high, weights[1], form, preferred_element_type=jnp.float32)
    return first[:rows] + (first[rows:] + second)


def kernel(
    nb, ni,
    vec_hbm, basis_hbm, near_hbm, trans_hbm, coup_hbm, top_hbm, upper_hbm,
    source_ref, target_ref, top_source_ref,
    out_ref,
    vec, basis, near, trans, coup, top, upper,
    halo_low, halo_high, tab_low, tab_self, tab_high, dup, roots, near_sum,
    basis_w, quad_w,
    local_sem, halo_send, halo_recv, leaf_send, leaf_recv, rest_send, rest_recv,
    root_send, root_recv, upper_send, upper_recv,
):
    cols, points = vec.shape
    rank = basis.shape[0]
    assert rank == 64 and near.shape[1] == 64
    wide = 2 * rank
    leaves = points // 64
    levels = leaves.bit_length() - 1
    starts = [2 * leaves - 2 * (leaves >> h) for h in range(levels + 1)]
    clusters = 2 * leaves - 1
    tiles = leaves
    half = leaves // 2
    slots = upper.shape[2] // rank
    n = nb * ni
    branch = lax.axis_index("branch")
    inner = lax.axis_index("inner")
    me = branch * ni + inner

    def place(index):
        return {"branch": index // ni, "inner": index % ni}

    loads = [
        pltpu.make_async_copy(vec_hbm, vec, local_sem.at[0]),
        pltpu.make_async_copy(basis_hbm, basis, local_sem.at[1]),
        pltpu.make_async_copy(upper_hbm, upper.at[branch, 0:rank], local_sem.at[2]),
        pltpu.make_async_copy(trans_hbm, trans, local_sem.at[3]),
        pltpu.make_async_copy(near_hbm, near, local_sem.at[4]),
        pltpu.make_async_copy(coup_hbm, coup, local_sem.at[5]),
        pltpu.make_async_copy(top_hbm, top, local_sem.at[6]),
    ]
    for load in loads:
        load.start()

    barrier = pltpu.get_barrier_semaphore()
    for step in range(1, n):
        pl.semaphore_signal(
            barrier, inc=1, device_id=place((me + step) % n), device_id_type=MESH
        )

    row = lax.broadcasted_iota(jnp.int32, (8, slots * rank), 0)
    lane = lax.broadcasted_iota(jnp.int32, (8, slots * rank), 1)
    meta = jnp.zeros((8, slots * rank), jnp.int32)
    for slot in range(slots):
        here = lane // rank == slot
        meta = jnp.where(here & (row == 0), target_ref[slot], meta)
        meta = jnp.where(here & (row == 1), top_source_ref[slot], meta)
    upper[branch, rank:, :] = meta.astype(jnp.float32)

    def to_high(source, target, send, recv):
        return pltpu.make_async_remote_copy(
            source, target, send.at[0], recv.at[0], device_id=place(me + 1), device_id_type=MESH
        )

    def to_low(source, target, send, recv):
        return pltpu.make_async_remote_copy(
            source, target, send.at[1], recv.at[1], device_id=place(me - 1), device_id_type=MESH
        )

    halo_copies = (
        to_high(vec.at[:, points - wide : points], halo_low, halo_send, halo_recv),
        to_low(vec.at[:, 0:wide], halo_high, halo_send, halo_recv),
    )
    leaf_copies = (
        to_high(tab_self.at[0:half], tab_low.at[0:half], leaf_send, leaf_recv),
        to_low(tab_self.at[0:half], tab_high.at[0:half], leaf_send, leaf_recv),
    )
    rest_copies = (
        to_high(tab_self.at[half:tiles], tab_low.at[half:tiles], rest_send, rest_recv),
        to_low(tab_self.at[half:tiles], tab_high.at[half:tiles], rest_send, rest_recv),
    )
    upper_copies = [
        pltpu.make_async_remote_copy(
            upper.at[branch], upper.at[branch], upper_send.at[step], upper_recv.at[step],
            device_id={"branch": (branch + step) % nb}, device_id_type=MESH,
        )
        for step in range(1, nb)
    ]
    root_copies = [
        pltpu.make_async_remote_copy(
            roots.at[me], roots.at[me], root_send.at[step], root_recv.at[step],
            device_id=place((me + step) % n), device_id_type=MESH,
        )
        for step in range(1, n)
    ]
    has_low = me > 0
    has_high = me < n - 1

    def start(copies):
        @pl.when(has_high)
        def _():
            copies[0].start()

        @pl.when(has_low)
        def _():
            copies[1].start()

    def arrived(copies):
        @pl.when(has_low)
        def _():
            copies[0].wait_recv()

        @pl.when(has_high)
        def _():
            copies[1].wait_recv()

    def sent(copies):
        @pl.when(has_high)
        def _():
            copies[0].wait_send()

        @pl.when(has_low)
        def _():
            copies[1].wait_send()

    low_64 = lax.broadcasted_iota(jnp.int32, (rank, wide), 1) < rank
    low_c = lax.broadcasted_iota(jnp.int32, (cols, wide), 1) < rank
    low_s = lax.broadcasted_iota(jnp.int32, (rank, 2 * wide), 1) < wide

    loads[0].wait()
    loads[1].wait()
    pairs = []
    for k in range(half):
        both = basis[:, k * wide : (k + 1) * wide]
        weights = split(
            jnp.concatenate([jnp.where(low_64, both, 0.0), jnp.where(low_64, 0.0, both)], axis=0)
        )
        basis_w[0, k] = weights[0]
        basis_w[1, k] = weights[1]
        pair = product(vec[:, k * wide : (k + 1) * wide], weights, NT)
        tab_self[k] = pair
        pairs.append(pair)

    pl.semaphore_wait(barrier, n - 1)
    start(halo_copies)
    start(leaf_copies)
    loads[2].wait()
    for copy in upper_copies:
        copy.start()

    loads[3].wait()
    quad = 0
    for h in range(levels - 1):
        breadth = leaves >> h
        base = starts[h] // 2
        lifted = []
        for j in range(breadth // 4):
            at = (base + 2 * j) * wide
            first = trans[:, at : at + wide]
            second = trans[:, at + wide : at + 2 * wide]
            weights = split(
                jnp.concatenate(
                    [
                        jnp.where(low_64, first, 0.0),
                        jnp.where(low_64, pltpu.roll(first, rank, 1), 0.0),
                        jnp.where(low_64, 0.0, pltpu.roll(second, rank, 1)),
                        jnp.where(low_64, 0.0, second),
                    ],
                    axis=0,
                )
            )
            quad_w[0, quad] = weights[0]
            quad_w[1, quad] = weights[1]
            quad += 1
            pair = product(
                jnp.concatenate([pairs[2 * j], pairs[2 * j + 1]], axis=1), weights, NN
            )
            tab_self[starts[h + 1] // 2 + j] = pair
            lifted.append(pair)
        pairs = lifted
    at = starts[levels - 1] * rank
    both = trans[:, at : at + wide]
    last_w = split(
        jnp.concatenate(
            [jnp.where(low_64, both, 0.0), jnp.where(low_64, pltpu.roll(both, rank, 1), 0.0)],
            axis=0,
        )
    )
    single = product(pairs[0], last_w, NN)
    tab_self[tiles - 1] = single
    root = trans[:, (clusters - 1) * rank : clusters * rank]
    root = jnp.concatenate([root, root], axis=1)
    root_w = split(jnp.concatenate([root, root], axis=0))
    roots[me] = product(single, root_w, NN)
    for copy in root_copies:
        copy.start()
    start(rest_copies)

    loads[4].wait()
    arrived(halo_copies)
    turned = [pltpu.roll(vec[:, k * wide : (k + 1) * wide], rank, 1) for k in range(half)]
    before = jnp.where(has_low, pltpu.roll(halo_low[...], rank, 1), 0.0)
    after = jnp.where(has_high, pltpu.roll(halo_high[...], rank, 1), 0.0)
    turned = [before] + turned + [after]
    shifted = [jnp.where(low_c, turned[k], turned[k + 1]) for k in range(half + 1)]
    for k in range(half):
        lanes = slice(k * wide, (k + 1) * wide)
        lower, middle, higher = near[0, :, lanes], near[1, :, lanes], near[2, :, lanes]
        weights = split(
            jnp.concatenate(
                [
                    jnp.where(low_64, lower, 0.0),
                    jnp.where(low_64, middle, lower),
                    jnp.where(low_64, higher, middle),
                    jnp.where(low_64, 0.0, higher),
                ],
                axis=0,
            )
        )
        near_sum[:, lanes] = product(
            jnp.concatenate([shifted[k], shifted[k + 1]], axis=1), weights, NN
        )

    def both_ways(table, offset):
        for k in range(tiles):
            tile = table[k]
            dup[offset + 2 * k] = tile
            dup[offset + 2 * k + 1] = pltpu.roll(tile, rank, 1)

    both_ways(tab_self, 2 * tiles)
    arrived(leaf_copies)
    arrived(rest_copies)

    @pl.when(has_low)
    def _():
        both_ways(tab_low, 0)

    @pl.when(has_high)
    def _():
        both_ways(tab_high, 4 * tiles)

    loads[5].wait()

    def gathered(q):
        h = max(i for i in range(levels + 1) if starts[i] <= q)
        shift = levels - h

        def entry(slot):
            c = source_ref[slot, q]
            run = lax.shift_right_logical(c, shift)
            side = jnp.clip(run - me + 1, 0, 2)
            return side * (2 * tiles) + starts[h] + (c - lax.shift_left(run, shift))

        second = entry(1)
        second = second + 1 - 2 * (second & 1)
        return jnp.where(low_c, dup[entry(0)], dup[second])

    coupled = []
    for k in range(tiles - 1):
        both = coup[:, 2 * k * wide : 2 * (k + 1) * wide]
        weights = split(
            jnp.concatenate([jnp.where(low_s, both, 0.0), jnp.where(low_s, 0.0, both)], axis=0)
        )
        x = jnp.concatenate([gathered(2 * k), gathered(2 * k + 1)], axis=1)
        coupled.append(product(x, weights, NT))
    one = coup[:, (clusters - 1) * wide : clusters * wide]
    coupled.append(
        product(gathered(clusters - 1), split(jnp.concatenate([one, one], axis=0)), NT)
    )

    loads[6].wait()
    top_w = []
    for k in range(nb // 2):
        both = top[:, k * wide : (k + 1) * wide]
        other = pltpu.roll(both, rank, 1)
        top_w.append(
            split(
                jnp.concatenate(
                    [jnp.where(low_64, both, other), jnp.where(low_64, other, both)], axis=0
                )
            )
        )
    own = top[:, pl.ds(pl.multiple_of((branch // 2) * wide, wide), wide)]
    own_w = split(jnp.concatenate([own, own], axis=0))
    for copy in upper_copies:
        copy.wait_recv()
    upper_w = []
    for s in range(nb):
        block = upper[s, 0:rank, :]
        upper_w.append(split(jnp.concatenate([block, block], axis=0)))
    for copy in root_copies:
        copy.wait_recv()
    xu = []
    for g in range(nb):
        total = roots[g * ni]
        for i in range(1, ni):
            total = total + roots[g * ni + i]
        xu.append(total)
    for k in range(nb // 2):
        xu.append(product(jnp.where(low_c, xu[2 * k], xu[2 * k + 1]), top_w[k], NN))
    xu = [jnp.concatenate([x] * (slots * rank // wide), axis=1) for x in xu]
    field = jnp.zeros((2 * cols, wide), jnp.float32)
    first_id = branch.astype(jnp.float32)
    second_id = (nb + branch // 2).astype(jnp.float32)
    for s in range(nb):
        target = upper[s, rank : rank + 1, :]
        source = upper[s, rank + 1 : rank + 2, :]
        chosen = jnp.zeros((cols, slots * rank), jnp.float32)
        for k, x in enumerate(xu):
            chosen = jnp.where(source == float(k), x, chosen)
        x = jnp.concatenate(
            [
                jnp.where(target == first_id, chosen, 0.0),
                jnp.where(target == second_id, chosen, 0.0),
            ],
            axis=0,
        )
        field = field + product(x, upper_w[s], NT)
    side = lax.broadcasted_iota(jnp.int32, (cols, wide), 1) // rank == branch % 2
    own_field = field[:cols] + product(jnp.where(side, field[cols:], 0.0), own_w, NT)

    state = coupled[tiles - 1] + product(jnp.where(low_c, own_field, 0.0), root_w, NT)
    pairs = [coupled[starts[levels - 1] // 2] + product(state, last_w, NT)]
    for h in reversed(range(levels - 1)):
        count = (leaves >> h) // 4
        quad -= count
        base = starts[h] // 2
        lowered = []
        for j in range(count):
            moved = product(pairs[j], (quad_w[0, quad + j], quad_w[1, quad + j]), NT)
            lowered.append(coupled[base + 2 * j] + moved[:, :wide])
            lowered.append(coupled[base + 2 * j + 1] + moved[:, wide:])
        pairs = lowered
    for k in range(half):
        lanes = slice(k * wide, (k + 1) * wide)
        out_ref[:, lanes] = near_sum[:, lanes] + product(
            pairs[k], (basis_w[0, k], basis_w[1, k]), NN
        )

    sent(halo_copies)
    sent(leaf_copies)
    sent(rest_copies)
    for copy in upper_copies + root_copies:
        copy.wait_send()


def on_device(
    vectors,
    leaf_basis,
    near_blocks,
    transfer,
    coupling,
    coupling_source,
    top_transfer,
    upper_coupling_matrices,
    top_target,
    top_source,
):
    cols, points = vectors.shape
    rank = leaf_basis.shape[0]
    leaf_len = near_blocks.shape[1]
    leaves = points // leaf_len
    nb = lax.axis_size("branch")
    ni = lax.axis_size("inner")
    n = nb * ni
    quads = sum((leaves >> h) // 4 for h in range(leaves.bit_length() - 2))
    wide = 2 * rank
    f32, bf16 = jnp.float32, jnp.bfloat16
    dma = pltpu.SemaphoreType.DMA
    hbm = pl.BlockSpec(memory_space=pltpu.HBM)
    smem = pl.BlockSpec(memory_space=pltpu.SMEM)
    table = pltpu.VMEM((leaves, cols, wide), f32)
    halo = pltpu.VMEM((cols, wide), f32)
    return pl.pallas_call(
        functools.partial(kernel, nb, ni),
        out_shape=jax.ShapeDtypeStruct((cols, points), f32),
        in_specs=[hbm] * 7 + [smem] * 3,
        out_specs=pl.BlockSpec(memory_space=pltpu.VMEM),
        scratch_shapes=[
            pltpu.VMEM(vectors.shape, f32),
            pltpu.VMEM(leaf_basis.shape, f32),
            pltpu.VMEM(near_blocks.shape, f32),
            pltpu.VMEM(transfer.shape, f32),
            pltpu.VMEM(coupling.shape, f32),
            pltpu.VMEM(top_transfer.shape, f32),
            pltpu.VMEM((nb, rank + 8, upper_coupling_matrices.shape[1]), f32),
            halo,
            halo,
            table,
            table,
            table,
            pltpu.VMEM((6 * leaves, cols, wide), f32),
            pltpu.VMEM((n, cols, wide), f32),
            pltpu.VMEM((cols, points), f32),
            pltpu.VMEM((2, leaves // 2, wide, wide), bf16),
            pltpu.VMEM((2, quads, 2 * wide, wide), bf16),
            dma((7,)),
            dma((2,)),
            dma((2,)),
            dma((2,)),
            dma((2,)),
            dma((2,)),
            dma((2,)),
            dma((n,)),
            dma((n,)),
            dma((nb,)),
            dma((nb,)),
        ],
        compiler_params=pltpu.CompilerParams(
            collective_id=0, has_side_effects=True, vmem_limit_bytes=60 * 1024 * 1024
        ),
    )(
        vectors,
        leaf_basis,
        near_blocks,
        transfer,
        coupling,
        top_transfer,
        upper_coupling_matrices,
        coupling_source.T,
        top_target,
        top_source,
    )


def solution(mesh):
    placed = (
        P("rhs", ("groups", "branch", "inner")),
        P(None, ("groups", "branch", "inner")),
        P(None, None, ("groups", "branch", "inner")),
        P(None, ("groups", "branch", "inner")),
        P(None, ("groups", "branch", "inner")),
        P(("groups", "branch", "inner"), None),
        P(None, "groups"),
        P(None, ("groups", "branch")),
        P(("groups", "branch")),
        P(("groups", "branch")),
    )
    return jax.shard_map(
        on_device,
        mesh=mesh,
        in_specs=placed,
        out_specs=P("rhs", ("groups", "branch", "inner")),
        check_vma=False,
    )
```

```python
import functools

import jax
import jax.numpy as jnp
from jax import lax
from jax.experimental import pallas as pl
from jax.experimental.pallas import tpu as pltpu
from jax.sharding import PartitionSpec as P

MESH = pl.DeviceIdType.MESH
NN = (((1,), (0,)), ((), ()))
NT = (((1,), (1,)), ((), ()))


def split(x):
    high = x.astype(jnp.bfloat16)
    return high, (x - high.astype(jnp.float32)).astype(jnp.bfloat16)


def product(x, weights, form):
    rows = x.shape[0]
    high, low = split(x)
    both = jnp.concatenate([high, low], axis=0)
    first = lax.dot_general(both, weights[0], form, preferred_element_type=jnp.float32)
    second = lax.dot_general(high, weights[1], form, preferred_element_type=jnp.float32)
    return first[:rows] + (first[rows:] + second)


def kernel(
    nb, ni,
    vec_hbm, basis_hbm, near_hbm, trans_hbm, coup_hbm, top_hbm, upper_hbm,
    source_ref, target_ref, top_source_ref,
    out_ref,
    vec, basis, near, trans, coup, top, upper,
    halo_low, halo_high, tab_low, tab_self, tab_high, dup, roots, near_sum,
    basis_w, quad_w, coup_w, parts, fields,
    local_sem, halo_send, halo_recv, table_send, table_recv,
    root_send, root_recv, field_send, field_recv,
):
    cols, points = vec.shape
    rank = basis.shape[0]
    assert rank == 64 and near.shape[1] == 64
    wide = 2 * rank
    leaves = points // 64
    levels = leaves.bit_length() - 1
    starts = [2 * leaves - 2 * (leaves >> h) for h in range(levels + 1)]
    clusters = 2 * leaves - 1
    tiles = leaves
    half = leaves // 2
    slots = upper.shape[1] // rank
    n = nb * ni
    branch = lax.axis_index("branch")
    inner = lax.axis_index("inner")
    me = branch * ni + inner

    def place(index):
        return {"branch": index // ni, "inner": index % ni}

    loads = [
        pltpu.make_async_copy(vec_hbm, vec, local_sem.at[0]),
        pltpu.make_async_copy(basis_hbm, basis, local_sem.at[1]),
        pltpu.make_async_copy(upper_hbm, upper, local_sem.at[2]),
        pltpu.make_async_copy(trans_hbm, trans, local_sem.at[3]),
        pltpu.make_async_copy(near_hbm, near, local_sem.at[4]),
        pltpu.make_async_copy(coup_hbm, coup, local_sem.at[5]),
        pltpu.make_async_copy(top_hbm, top, local_sem.at[6]),
    ]
    for load in loads:
        load.start()

    barrier = pltpu.get_barrier_semaphore()
    for step in range(1, n):
        pl.semaphore_signal(
            barrier, inc=1, device_id=place((me + step) % n), device_id_type=MESH
        )

    def to_high(source, target, send, recv):
        return pltpu.make_async_remote_copy(
            source, target, send.at[0], recv.at[0], device_id=place(me + 1), device_id_type=MESH
        )

    def to_low(source, target, send, recv):
        return pltpu.make_async_remote_copy(
            source, target, send.at[1], recv.at[1], device_id=place(me - 1), device_id_type=MESH
        )

    halo_copies = (
        to_high(vec.at[:, points - wide : points], halo_low, halo_send, halo_recv),
        to_low(vec.at[:, 0:wide], halo_high, halo_send, halo_recv),
    )
    table_copies = (
        to_high(tab_self, tab_low, table_send, table_recv),
        to_low(tab_self, tab_high, table_send, table_recv),
    )
    field_copies = [
        pltpu.make_async_remote_copy(
            parts.at[(branch + step) % nb], fields.at[branch],
            field_send.at[step], field_recv.at[step],
            device_id={"branch": (branch + step) % nb}, device_id_type=MESH,
        )
        for step in range(1, nb)
    ]
    root_copies = [
        pltpu.make_async_remote_copy(
            roots.at[me], roots.at[me], root_send.at[step], root_recv.at[step],
            device_id=place((me + step) % n), device_id_type=MESH,
        )
        for step in range(1, n)
    ]
    has_low = me > 0
    has_high = me < n - 1

    def start(copies):
        @pl.when(has_high)
        def _():
            copies[0].start()

        @pl.when(has_low)
        def _():
            copies[1].start()

    def arrived(copies):
        @pl.when(has_low)
        def _():
            copies[0].wait_recv()

        @pl.when(has_high)
        def _():
            copies[1].wait_recv()

    def sent(copies):
        @pl.when(has_high)
        def _():
            copies[0].wait_send()

        @pl.when(has_low)
        def _():
            copies[1].wait_send()

    low_64 = lax.broadcasted_iota(jnp.int32, (rank, wide), 1) < rank
    low_c = lax.broadcasted_iota(jnp.int32, (cols, wide), 1) < rank
    low_s = lax.broadcasted_iota(jnp.int32, (rank, 2 * wide), 1) < wide

    loads[0].wait()
    loads[1].wait()
    pairs = []
    for k in range(half):
        both = basis[:, k * wide : (k + 1) * wide]
        weights = split(
            jnp.concatenate([jnp.where(low_64, both, 0.0), jnp.where(low_64, 0.0, both)], axis=0)
        )
        basis_w[0, k] = weights[0]
        basis_w[1, k] = weights[1]
        pair = product(vec[:, k * wide : (k + 1) * wide], weights, NT)
        tab_self[k] = pair
        pairs.append(pair)

    loads[3].wait()
    quad = 0
    for h in range(levels - 1):
        breadth = leaves >> h
        base = starts[h] // 2
        lifted = []
        for j in range(breadth // 4):
            at = (base + 2 * j) * wide
            first = trans[:, at : at + wide]
            second = trans[:, at + wide : at + 2 * wide]
            weights = split(
                jnp.concatenate(
                    [
                        jnp.where(low_64, first, 0.0),
                        jnp.where(low_64, pltpu.roll(first, rank, 1), 0.0),
                        jnp.where(low_64, 0.0, pltpu.roll(second, rank, 1)),
                        jnp.where(low_64, 0.0, second),
                    ],
                    axis=0,
                )
            )
            quad_w[0, quad] = weights[0]
            quad_w[1, quad] = weights[1]
            quad += 1
            pair = product(
                jnp.concatenate([pairs[2 * j], pairs[2 * j + 1]], axis=1), weights, NN
            )
            tab_self[starts[h + 1] // 2 + j] = pair
            lifted.append(pair)
        pairs = lifted
    at = starts[levels - 1] * rank
    both = trans[:, at : at + wide]
    last_w = split(
        jnp.concatenate(
            [jnp.where(low_64, both, 0.0), jnp.where(low_64, pltpu.roll(both, rank, 1), 0.0)],
            axis=0,
        )
    )
    single = product(pairs[0], last_w, NN)
    tab_self[tiles - 1] = single
    root = trans[:, (clusters - 1) * rank : clusters * rank]
    root = jnp.concatenate([root, root], axis=1)
    root_w = split(jnp.concatenate([root, root], axis=0))
    roots[me] = product(single, root_w, NN)
    turned = [pltpu.roll(vec[:, k * wide : (k + 1) * wide], rank, 1) for k in range(half)]

    def dense(k, first, second):
        lanes = slice(k * wide, (k + 1) * wide)
        lower, middle, higher = near[0, :, lanes], near[1, :, lanes], near[2, :, lanes]
        weights = split(
            jnp.concatenate(
                [
                    jnp.where(low_64, lower, 0.0),
                    jnp.where(low_64, middle, lower),
                    jnp.where(low_64, higher, middle),
                    jnp.where(low_64, 0.0, higher),
                ],
                axis=0,
            )
        )
        near_sum[:, lanes] = product(jnp.concatenate([first, second], axis=1), weights, NN)

    shifted = [jnp.where(low_c, turned[k], turned[k + 1]) for k in range(half - 1)]
    loads[4].wait()
    for k in range(1, half - 1):
        dense(k, shifted[k - 1], shifted[k])

    def both_ways(table, offset):
        for k in range(tiles):
            tile = table[k]
            dup[offset + 2 * k] = tile
            dup[offset + 2 * k + 1] = pltpu.roll(tile, rank, 1)

    both_ways(tab_self, 2 * tiles)
    loads[5].wait()
    for k in range(tiles - 1):
        both = coup[:, 2 * k * wide : 2 * (k + 1) * wide]
        weights = split(
            jnp.concatenate([jnp.where(low_s, both, 0.0), jnp.where(low_s, 0.0, both)], axis=0)
        )
        coup_w[0, k] = weights[0]
        coup_w[1, k] = weights[1]
    one = coup[:, (clusters - 1) * wide : clusters * wide]
    one_w = split(jnp.concatenate([one, one], axis=0))
    loads[2].wait()
    loads[6].wait()
    top_w = []
    for k in range(nb // 2):
        both = top[:, k * wide : (k + 1) * wide]
        other = pltpu.roll(both, rank, 1)
        top_w.append(
            split(
                jnp.concatenate(
                    [jnp.where(low_64, both, other), jnp.where(low_64, other, both)], axis=0
                )
            )
        )
    own = top[:, pl.ds(pl.multiple_of((branch // 2) * wide, wide), wide)]
    own_w = split(jnp.concatenate([own, own], axis=0))
    block = upper[...]
    upper_w = split(jnp.concatenate([block, block], axis=0))
    lane = lax.broadcasted_iota(jnp.int32, (cols, slots * rank), 1) // rank
    target = jnp.zeros((cols, slots * rank), jnp.int32)
    source = target
    for slot in range(slots):
        target = jnp.where(lane == slot, target_ref[slot], target)
        source = jnp.where(lane == slot, top_source_ref[slot], source)

    pl.semaphore_wait(barrier, n - 1)
    for copy in root_copies:
        copy.start()
    start(halo_copies)
    start(table_copies)

    for copy in root_copies:
        copy.wait_recv()
    xu = []
    for g in range(nb):
        total = roots[g * ni]
        for i in range(1, ni):
            total = total + roots[g * ni + i]
        xu.append(total)
    for k in range(nb // 2):
        xu.append(product(jnp.where(low_c, xu[2 * k], xu[2 * k + 1]), top_w[k], NN))
    chosen = jnp.zeros((cols, slots * rank), jnp.float32)
    for k, x in enumerate(xu):
        x = jnp.concatenate([x] * (slots * rank // wide), axis=1)
        chosen = jnp.where(source == k, x, chosen)
    field = product(
        jnp.concatenate(
            [jnp.where(target == k, chosen, 0.0) for k in range(nb + nb // 2)], axis=0
        ),
        upper_w,
        NT,
    )
    for g in range(nb):
        second = nb + g // 2
        parts[g] = jnp.where(
            low_c, field[g * cols : (g + 1) * cols], field[second * cols : (second + 1) * cols]
        )
    for copy in field_copies:
        copy.start()

    arrived(halo_copies)
    before = jnp.where(has_low, pltpu.roll(halo_low[...], rank, 1), 0.0)
    after = jnp.where(has_high, pltpu.roll(halo_high[...], rank, 1), 0.0)
    dense(0, jnp.where(low_c, before, turned[0]), shifted[0])
    dense(half - 1, shifted[half - 2], jnp.where(low_c, turned[half - 1], after))

    arrived(table_copies)

    @pl.when(has_low)
    def _():
        both_ways(tab_low, 0)

    @pl.when(has_high)
    def _():
        both_ways(tab_high, 4 * tiles)

    def gathered(q):
        h = max(i for i in range(levels + 1) if starts[i] <= q)
        shift = levels - h

        def entry(slot):
            c = source_ref[slot, q]
            run = lax.shift_right_logical(c, shift)
            side = jnp.clip(run - me + 1, 0, 2)
            return side * (2 * tiles) + starts[h] + (c - lax.shift_left(run, shift))

        second = entry(1)
        second = second + 1 - 2 * (second & 1)
        return jnp.where(low_c, dup[entry(0)], dup[second])

    coupled = []
    for k in range(tiles - 1):
        x = jnp.concatenate([gathered(2 * k), gathered(2 * k + 1)], axis=1)
        coupled.append(product(x, (coup_w[0, k], coup_w[1, k]), NT))
    coupled.append(product(gathered(clusters - 1), one_w, NT))

    own_field = parts[branch]
    for copy in field_copies:
        copy.wait_recv()
    for step in range(1, nb):
        own_field = own_field + fields[(branch + nb - step) % nb]
    odd = branch % 2
    side = lax.broadcasted_iota(jnp.int32, (cols, wide), 1) // rank == odd
    upper_part = jnp.where(odd == 1, own_field, pltpu.roll(own_field, rank, 1))
    own_field = own_field + product(jnp.where(side, upper_part, 0.0), own_w, NT)

    state = coupled[tiles - 1] + product(jnp.where(low_c, own_field, 0.0), root_w, NT)
    pairs = [coupled[starts[levels - 1] // 2] + product(state, last_w, NT)]
    for h in reversed(range(levels - 1)):
        count = (leaves >> h) // 4
        quad -= count
        base = starts[h] // 2
        lowered = []
        for j in range(count):
            moved = product(pairs[j], (quad_w[0, quad + j], quad_w[1, quad + j]), NT)
            lowered.append(coupled[base + 2 * j] + moved[:, :wide])
            lowered.append(coupled[base + 2 * j + 1] + moved[:, wide:])
        pairs = lowered
    for k in range(half):
        lanes = slice(k * wide, (k + 1) * wide)
        out_ref[:, lanes] = near_sum[:, lanes] + product(
            pairs[k], (basis_w[0, k], basis_w[1, k]), NN
        )

    sent(halo_copies)
    sent(table_copies)
    for copy in field_copies + root_copies:
        copy.wait_send()


def on_device(
    vectors,
    leaf_basis,
    near_blocks,
    transfer,
    coupling,
    coupling_source,
    top_transfer,
    upper_coupling_matrices,
    top_target,
    top_source,
):
    cols, points = vectors.shape
    rank = leaf_basis.shape[0]
    leaf_len = near_blocks.shape[1]
    leaves = points // leaf_len
    nb = lax.axis_size("branch")
    ni = lax.axis_size("inner")
    n = nb * ni
    quads = sum((leaves >> h) // 4 for h in range(leaves.bit_length() - 2))
    wide = 2 * rank
    f32, bf16 = jnp.float32, jnp.bfloat16
    dma = pltpu.SemaphoreType.DMA
    hbm = pl.BlockSpec(memory_space=pltpu.HBM)
    smem = pl.BlockSpec(memory_space=pltpu.SMEM)
    table = pltpu.VMEM((leaves, cols, wide), f32)
    halo = pltpu.VMEM((cols, wide), f32)
    return pl.pallas_call(
        functools.partial(kernel, nb, ni),
        out_shape=jax.ShapeDtypeStruct((cols, points), f32),
        in_specs=[hbm] * 7 + [smem] * 3,
        out_specs=pl.BlockSpec(memory_space=pltpu.VMEM),
        scratch_shapes=[
            pltpu.VMEM(vectors.shape, f32),
            pltpu.VMEM(leaf_basis.shape, f32),
            pltpu.VMEM(near_blocks.shape, f32),
            pltpu.VMEM(transfer.shape, f32),
            pltpu.VMEM(coupling.shape, f32),
            pltpu.VMEM(top_transfer.shape, f32),
            pltpu.VMEM(upper_coupling_matrices.shape, f32),
            halo,
            halo,
            table,
            table,
            table,
            pltpu.VMEM((6 * leaves, cols, wide), f32),
            pltpu.VMEM((n, cols, wide), f32),
            pltpu.VMEM((cols, points), f32),
            pltpu.VMEM((2, leaves // 2, wide, wide), bf16),
            pltpu.VMEM((2, quads, 2 * wide, wide), bf16),
            pltpu.VMEM((2, leaves - 1, wide, 2 * wide), bf16),
            pltpu.VMEM((nb, cols, wide), f32),
            pltpu.VMEM((nb, cols, wide), f32),
            dma((7,)),
            dma((2,)),
            dma((2,)),
            dma((2,)),
            dma((2,)),
            dma((n,)),
            dma((n,)),
            dma((nb,)),
            dma((nb,)),
        ],
        compiler_params=pltpu.CompilerParams(
            collective_id=0, has_side_effects=True, vmem_limit_bytes=60 * 1024 * 1024
        ),
    )(
        vectors,
        leaf_basis,
        near_blocks,
        transfer,
        coupling,
        top_transfer,
        upper_coupling_matrices,
        coupling_source.T,
        top_target,
        top_source,
    )


def solution(mesh):
    placed = (
        P("rhs", ("groups", "branch", "inner")),
        P(None, ("groups", "branch", "inner")),
        P(None, None, ("groups", "branch", "inner")),
        P(None, ("groups", "branch", "inner")),
        P(None, ("groups", "branch", "inner")),
        P(("groups", "branch", "inner"), None),
        P(None, "groups"),
        P(None, ("groups", "branch")),
        P(("groups", "branch")),
        P(("groups", "branch")),
    )
    return jax.shard_map(
        on_device,
        mesh=mesh,
        in_specs=placed,
        out_specs=P("rhs", ("groups", "branch", "inner")),
        check_vma=False,
    )
```

```python
import functools

import jax
import jax.numpy as jnp
from jax import lax
from jax.experimental import pallas as pl
from jax.experimental.pallas import tpu as pltpu
from jax.sharding import PartitionSpec as P

MESH = pl.DeviceIdType.MESH
NN = (((1,), (0,)), ((), ()))
NT = (((1,), (1,)), ((), ()))


def split(x):
    high = x.astype(jnp.bfloat16)
    return high, (x - high.astype(jnp.float32)).astype(jnp.bfloat16)


def product(x, weights, form):
    rows = x.shape[0]
    high, low = split(x)
    both = jnp.concatenate([high, low], axis=0)
    first = lax.dot_general(both, weights[0], form, preferred_element_type=jnp.float32)
    second = lax.dot_general(high, weights[1], form, preferred_element_type=jnp.float32)
    return first[:rows] + (first[rows:] + second)


def kernel(
    nb, ni,
    vec_hbm, basis_hbm, near_hbm, trans_hbm, coup_hbm, top_hbm, upper_hbm,
    source_ref, target_ref, top_source_ref,
    out_ref,
    vec, basis, near, trans, coup, top, upper,
    halo_low, halo_high, tab_low, tab_self, tab_high, dup, roots, near_sum,
    basis_w, quad_w, coup_w, parts, fields,
    local_sem, halo_send, halo_recv, table_send, table_recv,
    root_send, root_recv, field_send, field_recv,
):
    cols, points = vec.shape
    rank = basis.shape[0]
    assert rank == 64 and near.shape[1] == 64
    wide = 2 * rank
    leaves = points // 64
    levels = leaves.bit_length() - 1
    starts = [2 * leaves - 2 * (leaves >> h) for h in range(levels + 1)]
    clusters = 2 * leaves - 1
    tiles = leaves
    half = leaves // 2
    slots = upper.shape[1] // rank
    n = nb * ni
    branch = lax.axis_index("branch")
    inner = lax.axis_index("inner")
    me = branch * ni + inner

    def place(index):
        return {"branch": index // ni, "inner": index % ni}

    loads = [
        pltpu.make_async_copy(vec_hbm, vec, local_sem.at[0]),
        pltpu.make_async_copy(basis_hbm, basis, local_sem.at[1]),
        pltpu.make_async_copy(upper_hbm, upper, local_sem.at[2]),
        pltpu.make_async_copy(trans_hbm, trans, local_sem.at[3]),
        pltpu.make_async_copy(near_hbm, near, local_sem.at[4]),
        pltpu.make_async_copy(coup_hbm, coup, local_sem.at[5]),
        pltpu.make_async_copy(top_hbm, top, local_sem.at[6]),
    ]
    barrier = pltpu.get_barrier_semaphore()
    for step in range(1, n):
        pl.semaphore_signal(
            barrier, inc=1, device_id=place((me + step) % n), device_id_type=MESH
        )
    for load in loads:
        load.start()

    def to_high(source, target, send, recv):
        return pltpu.make_async_remote_copy(
            source, target, send.at[0], recv.at[0], device_id=place(me + 1), device_id_type=MESH
        )

    def to_low(source, target, send, recv):
        return pltpu.make_async_remote_copy(
            source, target, send.at[1], recv.at[1], device_id=place(me - 1), device_id_type=MESH
        )

    halo_copies = (
        to_high(vec.at[:, points - wide : points], halo_low, halo_send, halo_recv),
        to_low(vec.at[:, 0:wide], halo_high, halo_send, halo_recv),
    )
    table_copies = (
        to_high(tab_self, tab_low, table_send, table_recv),
        to_low(tab_self, tab_high, table_send, table_recv),
    )
    field_copies = [
        pltpu.make_async_remote_copy(
            parts.at[(branch + step) % nb], fields.at[branch],
            field_send.at[step], field_recv.at[step],
            device_id={"branch": (branch + step) % nb}, device_id_type=MESH,
        )
        for step in range(1, nb)
    ]
    root_copies = [
        pltpu.make_async_remote_copy(
            roots.at[me], roots.at[me], root_send.at[step], root_recv.at[step],
            device_id=place((me + step) % n), device_id_type=MESH,
        )
        for step in range(1, n)
    ]
    has_low = me > 0
    has_high = me < n - 1

    def start(copies):
        @pl.when(has_high)
        def _():
            copies[0].start()

        @pl.when(has_low)
        def _():
            copies[1].start()

    def arrived(copies):
        @pl.when(has_low)
        def _():
            copies[0].wait_recv()

        @pl.when(has_high)
        def _():
            copies[1].wait_recv()

    def sent(copies):
        @pl.when(has_high)
        def _():
            copies[0].wait_send()

        @pl.when(has_low)
        def _():
            copies[1].wait_send()

    low_64 = lax.broadcasted_iota(jnp.int32, (rank, wide), 1) < rank
    low_c = lax.broadcasted_iota(jnp.int32, (cols, wide), 1) < rank
    low_s = lax.broadcasted_iota(jnp.int32, (rank, 2 * wide), 1) < wide

    loads[0].wait()
    loads[1].wait()
    pairs = []
    for k in range(half):
        both = basis[:, k * wide : (k + 1) * wide]
        weights = split(
            jnp.concatenate([jnp.where(low_64, both, 0.0), jnp.where(low_64, 0.0, both)], axis=0)
        )
        basis_w[0, k] = weights[0]
        basis_w[1, k] = weights[1]
        pair = product(vec[:, k * wide : (k + 1) * wide], weights, NT)
        tab_self[k] = pair
        pairs.append(pair)

    loads[3].wait()
    quad = 0
    for h in range(levels - 1):
        breadth = leaves >> h
        base = starts[h] // 2
        lifted = []
        for j in range(breadth // 4):
            at = (base + 2 * j) * wide
            first = trans[:, at : at + wide]
            second = trans[:, at + wide : at + 2 * wide]
            weights = split(
                jnp.concatenate(
                    [
                        jnp.where(low_64, first, 0.0),
                        jnp.where(low_64, pltpu.roll(first, rank, 1), 0.0),
                        jnp.where(low_64, 0.0, pltpu.roll(second, rank, 1)),
                        jnp.where(low_64, 0.0, second),
                    ],
                    axis=0,
                )
            )
            quad_w[0, quad] = weights[0]
            quad_w[1, quad] = weights[1]
            quad += 1
            pair = product(
                jnp.concatenate([pairs[2 * j], pairs[2 * j + 1]], axis=1), weights, NN
            )
            tab_self[starts[h + 1] // 2 + j] = pair
            lifted.append(pair)
        pairs = lifted
    at = starts[levels - 1] * rank
    both = trans[:, at : at + wide]
    last_w = split(
        jnp.concatenate(
            [jnp.where(low_64, both, 0.0), jnp.where(low_64, pltpu.roll(both, rank, 1), 0.0)],
            axis=0,
        )
    )
    single = product(pairs[0], last_w, NN)
    tab_self[tiles - 1] = single
    root = trans[:, (clusters - 1) * rank : clusters * rank]
    root = jnp.concatenate([root, root], axis=1)
    root_w = split(jnp.concatenate([root, root], axis=0))
    term = product(single, root_w, NN)
    part = cols // 2
    low_p = lax.broadcasted_iota(jnp.int32, (part, wide), 1) < rank
    roots[me] = jnp.where(low_p, term[:part], term[part:])
    turned = [pltpu.roll(vec[:, k * wide : (k + 1) * wide], rank, 1) for k in range(half)]

    def dense(k, first, second):
        lanes = slice(k * wide, (k + 1) * wide)
        lower, middle, higher = near[0, :, lanes], near[1, :, lanes], near[2, :, lanes]
        weights = split(
            jnp.concatenate(
                [
                    jnp.where(low_64, lower, 0.0),
                    jnp.where(low_64, middle, lower),
                    jnp.where(low_64, higher, middle),
                    jnp.where(low_64, 0.0, higher),
                ],
                axis=0,
            )
        )
        near_sum[:, lanes] = product(jnp.concatenate([first, second], axis=1), weights, NN)

    shifted = [jnp.where(low_c, turned[k], turned[k + 1]) for k in range(half - 1)]

    def both_ways(table, offset):
        for k in range(tiles):
            tile = table[k]
            dup[offset + 2 * k] = tile
            dup[offset + 2 * k + 1] = pltpu.roll(tile, rank, 1)

    both_ways(tab_self, 2 * tiles)
    loads[5].wait()
    for k in range(tiles - 1):
        both = coup[:, 2 * k * wide : 2 * (k + 1) * wide]
        weights = split(
            jnp.concatenate([jnp.where(low_s, both, 0.0), jnp.where(low_s, 0.0, both)], axis=0)
        )
        coup_w[0, k] = weights[0]
        coup_w[1, k] = weights[1]
    one = coup[:, (clusters - 1) * wide : clusters * wide]
    one_w = split(jnp.concatenate([one, one], axis=0))
    loads[2].wait()
    loads[6].wait()
    top_w = []
    for k in range(nb // 2):
        both = top[:, k * wide : (k + 1) * wide]
        other = pltpu.roll(both, rank, 1)
        top_w.append(
            split(
                jnp.concatenate(
                    [jnp.where(low_64, both, other), jnp.where(low_64, other, both)], axis=0
                )
            )
        )
    own = top[:, pl.ds(pl.multiple_of((branch // 2) * wide, wide), wide)]
    own_w = split(jnp.concatenate([own, own], axis=0))
    block = upper[...]
    upper_w = split(jnp.concatenate([block, block], axis=0))
    lane = lax.broadcasted_iota(jnp.int32, (cols, slots * rank), 1) // rank
    target = jnp.zeros((cols, slots * rank), jnp.int32)
    source = target
    for slot in range(slots):
        target = jnp.where(lane == slot, target_ref[slot], target)
        source = jnp.where(lane == slot, top_source_ref[slot], source)

    pl.semaphore_wait(barrier, n - 1)
    for copy in root_copies:
        copy.start()
    start(halo_copies)
    start(table_copies)

    for copy in root_copies:
        copy.wait_recv()
    xu = []
    for g in range(nb):
        total = roots[g * ni]
        for i in range(1, ni):
            total = total + roots[g * ni + i]
        other = pltpu.roll(total, rank, 1)
        xu.append(
            jnp.concatenate(
                [jnp.where(low_p, total, other), jnp.where(low_p, other, total)], axis=0
            )
        )
    for k in range(nb // 2):
        xu.append(product(jnp.where(low_c, xu[2 * k], xu[2 * k + 1]), top_w[k], NN))
    chosen = jnp.zeros((cols, slots * rank), jnp.float32)
    for k, x in enumerate(xu):
        x = jnp.concatenate([x] * (slots * rank // wide), axis=1)
        chosen = jnp.where(source == k, x, chosen)
    field = product(
        jnp.concatenate(
            [jnp.where(target == k, chosen, 0.0) for k in range(nb + nb // 2)], axis=0
        ),
        upper_w,
        NT,
    )
    for g in range(nb):
        second = nb + g // 2
        parts[g] = jnp.where(
            low_c, field[g * cols : (g + 1) * cols], field[second * cols : (second + 1) * cols]
        )
    for copy in field_copies:
        copy.start()

    loads[4].wait()
    for k in range(1, half - 1):
        dense(k, shifted[k - 1], shifted[k])
    arrived(halo_copies)
    before = jnp.where(has_low, pltpu.roll(halo_low[...], rank, 1), 0.0)
    after = jnp.where(has_high, pltpu.roll(halo_high[...], rank, 1), 0.0)
    dense(0, jnp.where(low_c, before, turned[0]), shifted[0])
    dense(half - 1, shifted[half - 2], jnp.where(low_c, turned[half - 1], after))

    arrived(table_copies)

    @pl.when(has_low)
    def _():
        both_ways(tab_low, 0)

    @pl.when(has_high)
    def _():
        both_ways(tab_high, 4 * tiles)

    def gathered(q):
        h = max(i for i in range(levels + 1) if starts[i] <= q)
        shift = levels - h

        def entry(slot):
            c = source_ref[slot, q]
            run = lax.shift_right_logical(c, shift)
            side = jnp.clip(run - me + 1, 0, 2)
            return side * (2 * tiles) + starts[h] + (c - lax.shift_left(run, shift))

        second = entry(1)
        second = second + 1 - 2 * (second & 1)
        return jnp.where(low_c, dup[entry(0)], dup[second])

    coupled = []
    for k in range(tiles - 1):
        x = jnp.concatenate([gathered(2 * k), gathered(2 * k + 1)], axis=1)
        coupled.append(product(x, (coup_w[0, k], coup_w[1, k]), NT))
    coupled.append(product(gathered(clusters - 1), one_w, NT))

    own_field = parts[branch]
    for copy in field_copies:
        copy.wait_recv()
    for step in range(1, nb):
        own_field = own_field + fields[(branch + nb - step) % nb]
    odd = branch % 2
    side = lax.broadcasted_iota(jnp.int32, (cols, wide), 1) // rank == odd
    upper_part = jnp.where(odd == 1, own_field, pltpu.roll(own_field, rank, 1))
    own_field = own_field + product(jnp.where(side, upper_part, 0.0), own_w, NT)

    state = coupled[tiles - 1] + product(jnp.where(low_c, own_field, 0.0), root_w, NT)
    pairs = [coupled[starts[levels - 1] // 2] + product(state, last_w, NT)]
    for h in reversed(range(levels - 1)):
        count = (leaves >> h) // 4
        quad -= count
        base = starts[h] // 2
        lowered = []
        for j in range(count):
            moved = product(pairs[j], (quad_w[0, quad + j], quad_w[1, quad + j]), NT)
            lowered.append(coupled[base + 2 * j] + moved[:, :wide])
            lowered.append(coupled[base + 2 * j + 1] + moved[:, wide:])
        pairs = lowered
    for k in range(half):
        lanes = slice(k * wide, (k + 1) * wide)
        out_ref[:, lanes] = near_sum[:, lanes] + product(
            pairs[k], (basis_w[0, k], basis_w[1, k]), NN
        )

    sent(halo_copies)
    sent(table_copies)
    for copy in field_copies + root_copies:
        copy.wait_send()


def on_device(
    vectors,
    leaf_basis,
    near_blocks,
    transfer,
    coupling,
    coupling_source,
    top_transfer,
    upper_coupling_matrices,
    top_target,
    top_source,
):
    cols, points = vectors.shape
    rank = leaf_basis.shape[0]
    leaf_len = near_blocks.shape[1]
    leaves = points // leaf_len
    nb = lax.axis_size("branch")
    ni = lax.axis_size("inner")
    n = nb * ni
    quads = sum((leaves >> h) // 4 for h in range(leaves.bit_length() - 2))
    wide = 2 * rank
    f32, bf16 = jnp.float32, jnp.bfloat16
    dma = pltpu.SemaphoreType.DMA
    hbm = pl.BlockSpec(memory_space=pltpu.HBM)
    smem = pl.BlockSpec(memory_space=pltpu.SMEM)
    table = pltpu.VMEM((leaves, cols, wide), f32)
    halo = pltpu.VMEM((cols, wide), f32)
    return pl.pallas_call(
        functools.partial(kernel, nb, ni),
        out_shape=jax.ShapeDtypeStruct((cols, points), f32),
        in_specs=[hbm] * 7 + [smem] * 3,
        out_specs=pl.BlockSpec(memory_space=pltpu.VMEM),
        scratch_shapes=[
            pltpu.VMEM(vectors.shape, f32),
            pltpu.VMEM(leaf_basis.shape, f32),
            pltpu.VMEM(near_blocks.shape, f32),
            pltpu.VMEM(transfer.shape, f32),
            pltpu.VMEM(coupling.shape, f32),
            pltpu.VMEM(top_transfer.shape, f32),
            pltpu.VMEM(upper_coupling_matrices.shape, f32),
            halo,
            halo,
            table,
            table,
            table,
            pltpu.VMEM((6 * leaves, cols, wide), f32),
            pltpu.VMEM((n, cols // 2, wide), f32),
            pltpu.VMEM((cols, points), f32),
            pltpu.VMEM((2, leaves // 2, wide, wide), bf16),
            pltpu.VMEM((2, quads, 2 * wide, wide), bf16),
            pltpu.VMEM((2, leaves - 1, wide, 2 * wide), bf16),
            pltpu.VMEM((nb, cols, wide), f32),
            pltpu.VMEM((nb, cols, wide), f32),
            dma((7,)),
            dma((2,)),
            dma((2,)),
            dma((2,)),
            dma((2,)),
            dma((n,)),
            dma((n,)),
            dma((nb,)),
            dma((nb,)),
        ],
        compiler_params=pltpu.CompilerParams(
            collective_id=0, has_side_effects=True, vmem_limit_bytes=60 * 1024 * 1024
        ),
    )(
        vectors,
        leaf_basis,
        near_blocks,
        transfer,
        coupling,
        top_transfer,
        upper_coupling_matrices,
        coupling_source.T,
        top_target,
        top_source,
    )


def solution(mesh):
    placed = (
        P("rhs", ("groups", "branch", "inner")),
        P(None, ("groups", "branch", "inner")),
        P(None, None, ("groups", "branch", "inner")),
        P(None, ("groups", "branch", "inner")),
        P(None, ("groups", "branch", "inner")),
        P(("groups", "branch", "inner"), None),
        P(None, "groups"),
        P(None, ("groups", "branch")),
        P(("groups", "branch")),
        P(("groups", "branch")),
    )
    return jax.shard_map(
        on_device,
        mesh=mesh,
        in_specs=placed,
        out_specs=P("rhs", ("groups", "branch", "inner")),
        check_vma=False,
    )
```
